32 devices in a mesh: dp: 8 (over z, x), fsdp: 4 (over y, core).
Axes of the slice: x: 2, y: 2, z: 4, core: 2. Of those that a mesh axis runs over, the one named last changes fastest.
Arguments:
- tokens: bfloat16 [16384, 768], P(('dp', 'fsdp')), may hold values from -6 to 6
- attn_gain: bfloat16 [768], P(('dp', 'fsdp')), may hold values from 0.5 to 1.5
- qkv_weight: bfloat16 [768, 2304], P(('dp', 'fsdp')), may hold values from -0.109375 to 0.109375
- out_weight: bfloat16 [768, 768], P(('dp', 'fsdp')), may hold values from -1.75 to 1.75
- ffn_gain: bfloat16 [768], P(('dp', 'fsdp')), may hold values from 0.5 to 1.5
- router_weight: bfloat16 [768, 2], P(('dp', 'fsdp')), may hold values from -0.15625 to 0.15625
- inner_weight: bfloat16 [2, 768, 6144], P(None, ('dp', 'fsdp')), may hold values from -0.21875 to 0.21875
- outer_weight: bfloat16 [2, 3072, 768], P(None, ('dp', 'fsdp')), may hold values from -0.3125 to 0.3125
- bias_table: float32 [32, 12], replicated, may hold values from -5 to 5
- lengths: int32 [32, 4], P(('dp', 'fsdp')), may hold values from 0 to 512, as said below
- routes: int32 [16384, 1], P(('dp', 'fsdp')), may hold values from 0 to 1; in each aligned block of 512 rows (0 to 511, 512 to 1023, ...) at most 320 rows name the same one
- buckets: int32 [1023], replicated, may hold values from 0 to 31, as said below
- out_cotangent: bfloat16 [16384, 768], P(('dp', 'fsdp')), may hold values from -6 to 6
Outputs:
- mixed: bfloat16 [16384, 768], P(('dp', 'fsdp'))
- tokens_grad: float32 [16384, 768], P(('dp', 'fsdp'))
- attn_gain_grad: float32 [768], P(('dp', 'fsdp'))
- qkv_weight_grad: float32 [768, 2304], P(('dp', 'fsdp'))
- out_weight_grad: float32 [768, 768], P(('dp', 'fsdp'))
- ffn_gain_grad: float32 [768], P(('dp', 'fsdp'))
- router_grad: float32 [768, 2], P(('dp', 'fsdp'))
- inner_grad: float32 [2, 768, 6144], P(None, ('dp', 'fsdp'))
- outer_grad: float32 [2, 3072, 768], P(None, ('dp', 'fsdp'))
- table_grad: float32 [32, 12], replicated
The draws below stay inside these ranges and needn't reach their ends.
Inputs may be any that keep to these rules, and one draw needn't show every extreme that they name: `lengths`: each row sums to at least 256 and at most 512; a length may be 0. In every draw some row holds a single sequence of 512 tokens. `routes`: among the rows of one device no expert is named by more than 320 rows, a bound that some block reaches. Entry o is the bucket of relative offset o - 511; buckets 0 to 15 serve offsets 0 and below, the rest positive offsets, and on either side the bucket does not fall as the distance grows.
All inputs are finite; a program needn't handle non-finite values.
Results may differ from the reference program's by a relative error of at most 0.015.
The reference program's roundings to bfloat16 on the way count: a program that leaves them out, or rounds other values in their place, can miss the bound.
Values may be sent and summed in bfloat16 or wider, within the bound.
A program may use at most 256 MiB of HBM per device.

```python
import math
import jax
import jax.numpy as jnp
import numpy as np
from jax import lax

D = 768
HEADS = 12
HEAD_DIM = 64
FF = 3072
BUCKETS = 32
EXPERTS = 2
SEQ_DEV = 4
TOK_DEV = 512
CAP = 320
TOKENS = 16384
DEVICES = 32


def draw_lengths(key, part):
    key = jax.random.fold_in(key, 11)
    live_key, cut_key, full_key = jax.random.split(key, 3)
    live_count = jax.random.randint(live_key, (DEVICES, 1), TOK_DEV // 2, TOK_DEV + 1)
    cut_points = jax.random.randint(cut_key, (DEVICES, SEQ_DEV - 1), 0, live_count + 1)
    cut_points = jnp.sort(cut_points, axis=1)
    bounds = jnp.concatenate([jnp.zeros((DEVICES, 1), jnp.int32), cut_points.astype(jnp.int32), live_count.astype(jnp.int32)], axis=1)
    seq_spans = bounds[:, 1:] - bounds[:, :-1]
    full_row = jax.random.randint(full_key, (), 0, DEVICES)
    single = jnp.zeros((SEQ_DEV,), jnp.int32).at[0].set(TOK_DEV)
    rows_id = jnp.arange(DEVICES, dtype=jnp.int32)
    return jnp.where((rows_id == full_row)[:, None], single[None, :], seq_spans).astype(jnp.int32)


def bucket_limits(side_key):
    half_count = BUCKETS // 2
    exact_count = half_count // 2
    place_idx = jnp.arange(half_count - 1, dtype=jnp.int32)
    upper_step = jnp.where(place_idx < exact_count, 4, 2 ** (jnp.maximum(place_idx - exact_count, 0) + 2) + 1)
    drawn_steps = jax.random.randint(side_key, (half_count - 1,), 1, upper_step)
    cumulative = jnp.cumsum(drawn_steps.astype(jnp.int32)).astype(jnp.int32)
    return jnp.minimum(cumulative, TOK_DEV - half_count + 1 + place_idx).astype(jnp.int32)


def draw_buckets(key, part):
    key = jax.random.fold_in(key, 23)
    below_key, above_key = jax.random.split(key, 2)
    half_count = BUCKETS // 2
    below_limits = bucket_limits(below_key)
    above_limits = bucket_limits(above_key)
    offset = jnp.arange(2 * TOK_DEV - 1, dtype=jnp.int32) - (TOK_DEV - 1)
    distance = jnp.abs(offset)
    above = offset > 0
    limits = jnp.where(above[:, None], above_limits[None, :], below_limits[None, :])
    count_below = jnp.sum((limits <= distance[:, None]).astype(jnp.int32), axis=1)
    return (count_below + half_count * above.astype(jnp.int32)).astype(jnp.int32)


def block_scale(key, dims, cuts, least, top_value):
    level, own = 1.0, jax.random.fold_in(key, 6)
    for dim, blocks in cuts:
        steps = jnp.exp(jax.random.uniform(jax.random.fold_in(own, dim), (blocks,), jnp.float32, least / len(cuts), top_value / len(cuts)))
        level = level * jnp.repeat(steps, dims[dim] // blocks).reshape([-1 if axis == dim else 1 for axis in range(len(dims))])
    return level


def shared_out(own_key, own, number, rows, number_of, top, bound, skew):
    sequence = jax.random.permutation(own_key, number_of)
    packed, ordinary = shares(number_of, rows * top, bound, skew, True), shares(number_of, rows * top, bound, skew, False)
    places = jnp.arange(number_of)

    def named(sizes, offset_by):
        used = int((sizes > 0).sum())
        fixed = max(1, used // 4)
        moved = fixed + (places - fixed + offset_by * (used - fixed)) % max(1, number_of - fixed)
        return jnp.zeros((number_of,), jnp.int32).at[sequence[jnp.where(places < fixed, places, moved)]].set(jnp.asarray(sizes, jnp.int32))

    sizes = jnp.where(number % 4 == 0, named(packed, number // 4), named(ordinary, number - number // 4 - 1))
    mixed = jax.random.permutation(jax.random.fold_in(own, 3), number_of)
    giver, receiver = mixed[0:number_of // 2 * 2:2], mixed[1:number_of // 2 * 2:2]
    slack = jnp.minimum(sizes[giver] - 1, bound - sizes[receiver]) // 2
    slack = jnp.where((giver == sequence[0]) | (receiver == sequence[0]) | (sizes[receiver] == 0), 0, jnp.maximum(slack, 0))
    moved = jax.random.randint(jax.random.fold_in(own, 4), (number_of // 2,), 0, 1 << 20) % (slack + 1)
    sizes = sizes.at[giver].add(-moved).at[receiver].add(moved)
    members = jnp.searchsorted(jnp.cumsum(sizes), jnp.arange(rows * top), side="right").astype(jnp.int32)
    table = members.reshape(top, rows).T
    table = table[jax.random.permutation(jax.random.fold_in(own, 1), rows)]
    offset_by = jax.random.randint(jax.random.fold_in(own, 2), (rows, 1), 0, top)
    return jnp.take_along_axis(table, (jnp.arange(top)[None, :] + offset_by) % top, axis=1)


def shares(number_of, total, reach, skew, full):
    portions = [(1 << 20) // math.isqrt(rank ** skew) + 1 for rank in range(1, number_of + 1)]
    largest = reach if full else min(reach, max(-(-total // number_of), total * portions[0] // sum(portions)))
    least = 1 if total - largest >= number_of - 1 else 0
    holding, rest = [largest] + [least] * (number_of - 1), total - largest - least * (number_of - 1)
    while rest > 0:
        candidates = [i for i in range(1, number_of) if holding[i] < largest] or [i for i in range(1, number_of) if holding[i] < reach]
        whole, budget = sum([portions[i] for i in candidates]), rest
        for i in candidates:
            more = min(reach - holding[i], max(1, budget * portions[i] // whole), rest)
            holding[i] = holding[i] + more
            rest = rest - more
    return np.array(holding)


def centred(rng, shape, spread, limit, shards=(), kind=jnp.bfloat16):
    loudness = block_scale(rng, shape, shards, -0.22, 0.18) if shards else 1.0
    entries = jax.random.normal(rng, shape, jnp.float32) * spread * loudness
    return jnp.minimum(jnp.maximum(entries, -limit), limit).astype(kind)


def setup_inputs(seed: int = 0) -> dict:
    splits = jax.random.split(jax.random.key(seed), 14)
    tokens = centred(splits[0], (TOKENS, D), 1.0, 6.0, ((0, 32),))
    attn_gain = jnp.clip(1.0 + 0.1 * jax.random.normal(splits[1], (D,), jnp.float32), 0.5, 1.5).astype(jnp.bfloat16)
    qkv_weight = centred(splits[2], (D, 3 * D), (4 * D) ** -0.5, 0.109375, ((0, 32),))
    out_weight = centred(splits[3], (D, D), (D // 64) ** -0.5, 1.75, ((0, 32),))
    ffn_gain = jnp.clip(1.0 + 0.1 * jax.random.normal(splits[4], (D,), jnp.float32), 0.5, 1.5).astype(jnp.bfloat16)
    router_weight = centred(splits[5], (D, EXPERTS), (2 * D) ** -0.5, 0.15625, ((0, 32),))
    inner_weight = centred(splits[6], (EXPERTS, D, 2 * FF), D ** -0.5, 0.21875, ((1, 32),))
    outer_weight = centred(splits[7], (EXPERTS, FF, D), (FF // 8) ** -0.5, 0.3125, ((1, 32),))
    bias_table = centred(splits[8], (BUCKETS, HEADS), 1.0, 5.0, (), jnp.float32)
    lengths = draw_lengths(jax.random.fold_in(splits[13], 71), 0)
    routes_keys = jax.random.split(jax.random.fold_in(splits[10], 1), TOKENS // TOK_DEV)
    routes_turns = jax.random.permutation(jax.random.fold_in(splits[10], 3), TOKENS // TOK_DEV)
    routes = jax.vmap(lambda own, number: shared_out(jax.random.fold_in(splits[10], 2), own, number, TOK_DEV, EXPERTS, 1, CAP, 1))(routes_keys, routes_turns).reshape((TOKENS, 1))
    buckets = draw_buckets(jax.random.fold_in(splits[13], 71), 0)
    out_cotangent = centred(splits[12], (TOKENS, D), 1.0, 6.0, ((0, 32),))
    return dict(tokens=tokens, attn_gain=attn_gain, qkv_weight=qkv_weight, out_weight=out_weight, ffn_gain=ffn_gain, router_weight=router_weight, inner_weight=inner_weight, outer_weight=outer_weight, bias_table=bias_table, lengths=lengths, routes=routes, buckets=buckets, out_cotangent=out_cotangent)


EPSILON = 1e-06
NEGATIVE = -1e+30
HIGHEST = lax.Precision.HIGHEST

@jax.custom_vjp
def low(v):
    return lax.optimization_barrier(v.astype(jnp.bfloat16)).astype(jnp.float32)

@jax.custom_vjp
def low_back(v):
    return v

def low_keep(v):
    return (low(v), None)

def low_pass(kept, grad):
    return (grad,)

def back_keep(v):
    return (v, None)

def back_low(kept, grad):
    return (low(grad),)
low.defvjp(low_keep, low_pass)
low_back.defvjp(back_keep, back_low)

def dot_high(left_side, right_side):
    return jnp.dot(left_side, right_side, precision=HIGHEST, preferred_element_type=jnp.float32)

def rms_scale(values, gain_row):
    return values * lax.rsqrt(lax.optimization_barrier(jnp.mean(values * values, axis=-1, keepdims=True)) + EPSILON) * gain_row

def softmax_rows(scores):
    highest = lax.optimization_barrier(jnp.max(scores, axis=-1, keepdims=True))
    raised = jnp.exp(scores - highest)
    return raised / lax.optimization_barrier(jnp.sum(raised, axis=-1, keepdims=True))

def segment_ids(lengths_row):
    seq_ends = jnp.cumsum(lengths_row).astype(jnp.int32)
    position = jnp.arange(TOK_DEV, dtype=jnp.int32)
    segment = lax.optimization_barrier(jnp.sum((position[:, None] >= seq_ends[None, :]).astype(jnp.int32), axis=1)).astype(jnp.int32)
    live_rows = (position < seq_ends[-1]).astype(jnp.float32)
    return (segment, live_rows)

def device_layer(params, tokens_in, route_col, segment, live_rows, offset_bucket):
    gain_one, qkv_weight, out_weight, gain_two, router_weight, inner_weight, outer_weight, table_full = params
    normed = low(rms_scale(tokens_in, gain_one))
    projected = low_back(low(dot_high(normed, qkv_weight)))
    queries = projected[:, :D].reshape(TOK_DEV, HEADS, HEAD_DIM)
    key_rows = projected[:, D:2 * D].reshape(TOK_DEV, HEADS, HEAD_DIM)
    value_rows = projected[:, 2 * D:].reshape(TOK_DEV, HEADS, HEAD_DIM)
    scores = jnp.einsum('qhd,khd->hqk', queries, key_rows, precision=HIGHEST)
    position_bias = jnp.transpose(table_full[offset_bucket], (2, 0, 1))
    scores = low_back(scores + position_bias)
    same_doc = segment[:, None] == segment[None, :]
    weights_low = low(softmax_rows(jnp.where(same_doc[None], scores, NEGATIVE)))
    context = jnp.einsum('hqk,khd->qhd', weights_low, value_rows, precision=HIGHEST).reshape(TOK_DEV, D)
    context = low_back(low(context))
    attended = low_back(dot_high(context, out_weight))
    middle = tokens_in + live_rows[:, None] * attended
    normed_two = low(rms_scale(middle, gain_two))
    router_probs = softmax_rows(dot_high(normed_two, router_weight))
    chosen = (route_col[:, None] == jnp.arange(EXPERTS, dtype=jnp.int32)[None, :]).astype(jnp.float32)
    gating = lax.optimization_barrier(jnp.sum(router_probs * chosen, axis=1))
    combined = jnp.zeros_like(tokens_in)
    for expert in range(EXPERTS):
        gate_up = low_back(dot_high(normed_two, inner_weight[expert]))
        activated = low(jax.nn.gelu(gate_up[:, :FF], approximate=True) * gate_up[:, FF:])
        expert_out = low_back(dot_high(activated, outer_weight[expert]))
        combined = combined + chosen[:, expert:expert + 1] * expert_out
    return middle + live_rows[:, None] * gating[:, None] * combined

def reference(tokens, attn_gain, qkv_weight, out_weight, ffn_gain, router_weight, inner_weight, outer_weight, bias_table, lengths, routes, buckets, out_cotangent):
    params = (attn_gain.astype(jnp.float32), qkv_weight.astype(jnp.float32), out_weight.astype(jnp.float32), ffn_gain.astype(jnp.float32), router_weight.astype(jnp.float32), inner_weight.astype(jnp.float32), outer_weight.astype(jnp.float32), bias_table.astype(jnp.float32))
    inputs = tokens.astype(jnp.float32).reshape(DEVICES, TOK_DEV, D)
    segments_all, live_all = jax.vmap(segment_ids)(lengths)
    route_rows = routes.reshape(DEVICES, TOK_DEV)
    position = jnp.arange(TOK_DEV, dtype=jnp.int32)
    offset_bucket = buckets[position[None, :] - position[:, None] + TOK_DEV - 1]
    layer_block = jax.checkpoint(device_layer)

    def forward(params_in, inputs_in):

        def one_device(device_item):
            return layer_block(params_in, device_item[0], device_item[1], device_item[2], device_item[3], offset_bucket)
        return lax.map(one_device, (inputs_in, route_rows, segments_all, live_all))
    outputs, pullback = jax.vjp(forward, params, inputs)
    param_grads, input_grad = pullback(out_cotangent.astype(jnp.float32).reshape(DEVICES, TOK_DEV, D))
    mixed = outputs.reshape(TOKENS, D).astype(jnp.bfloat16)
    return (mixed, input_grad.reshape(TOKENS, D), param_grads[0], param_grads[1], param_grads[2], param_grads[3], param_grads[4], param_grads[5], param_grads[6], param_grads[7])
```

```python
import jax
import jax.numpy as jnp
from jax import lax
from jax.experimental import pallas as pl
from jax.experimental.pallas import tpu as pltpu
from jax.sharding import PartitionSpec as P

CAP = 320
HEAD_DIM = 64


EPSILON = 1e-06
NEGATIVE = -1e30
HIGHEST = lax.Precision.HIGHEST


def rms_scale(values, gain_row):
    return (
        values * lax.rsqrt(jnp.mean(values * values, axis=-1, keepdims=True) + EPSILON) * gain_row
    )


def gated_unit(gate_up):
    hidden_units = gate_up.shape[-1] // 2
    return jax.nn.gelu(gate_up[..., :hidden_units], approximate=True) * gate_up[..., hidden_units:]


def contract_rows(left_side, right_side):
    return lax.dot_general(
        left_side, right_side, (((0,), (0,)), ((), ())), preferred_element_type=jnp.float32
    )


def contract_cols(left_side, right_side):
    return lax.dot_general(
        left_side, right_side, (((1,), (1,)), ((), ())), preferred_element_type=jnp.float32
    )


def head_lanes(values, head):
    lane = lax.broadcasted_iota(jnp.int32, values.shape, 1)
    return jnp.where((lane // HEAD_DIM) == head, values, jnp.zeros_like(values))


def forward_kernel(query_ref, key_ref, value_ref, offset_ref, seg_col_ref, seg_row_ref, context_ref, weight_ref):
    rows = query_ref.shape[0]
    same_doc = seg_col_ref[...] == seg_row_ref[...]
    query, key, value = query_ref[...], key_ref[...], value_ref[...]
    context = None
    for head in range(2):
        wide = jnp.broadcast_to(offset_ref[0, head : head + 1, :], (rows, 2 * rows))
        bias = pltpu.roll(wide, rows + 1, 1, stride=1, stride_axis=0)[:, :rows]
        scores = contract_cols(head_lanes(query, head), key) + bias
        scores = jnp.where(same_doc, scores, NEGATIVE)
        highest = jnp.max(scores, axis=-1, keepdims=True)
        raised = jnp.exp(scores - highest)
        weights = raised / jnp.sum(raised, axis=-1, keepdims=True)
        weight_ref[head] = weights
        part = jnp.dot(weights.astype(jnp.bfloat16), value, preferred_element_type=jnp.float32)
        part = head_lanes(part, head)
        context = part if context is None else context + part
    context_ref[...] = context.astype(jnp.bfloat16)


def attend_forward(projected, offset_pad, segment):
    rows, width = projected.shape
    groups = width // 3 // 128
    col = lambda part: pl.BlockSpec((rows, 128), lambda g: (0, part * groups + g))
    return pl.pallas_call(
        forward_kernel,
        grid=(groups,),
        in_specs=[
            col(0),
            col(1),
            col(2),
            pl.BlockSpec((1, 2, 2 * rows), lambda g: (g, 0, 0)),
            pl.BlockSpec((rows, 1), lambda g: (0, 0)),
            pl.BlockSpec((1, rows), lambda g: (0, 0)),
        ],
        out_specs=[
            pl.BlockSpec((rows, 128), lambda g: (0, g)),
            pl.BlockSpec((2, rows, rows), lambda g: (g, 0, 0)),
        ],
        out_shape=[
            jax.ShapeDtypeStruct((rows, width // 3), jnp.bfloat16),
            jax.ShapeDtypeStruct((2 * groups, rows, rows), jnp.float32),
        ],
        compiler_params=pltpu.CompilerParams(vmem_limit_bytes=48 * 1024 * 1024),
        cost_estimate=pl.CostEstimate(
            flops=8 * groups * rows * rows * 128, bytes_accessed=2**24, transcendentals=2**22
        ),
    )(
        projected,
        projected,
        projected,
        offset_pad.reshape(groups, 2, 2 * rows),
        segment[:, None],
        segment[None, :],
    )


def backward_kernel(
    query_ref, key_ref, value_ref, grad_ref, weight_ref, dq_ref, dk_ref, dv_ref, offset_ref
):
    rows = query_ref.shape[0]
    query, key, value, grad = query_ref[...], key_ref[...], value_ref[...], grad_ref[...]
    row_id = lax.broadcasted_iota(jnp.int32, (rows, rows), 0)
    col_id = lax.broadcasted_iota(jnp.int32, (rows, rows), 1)
    flip = jnp.where(row_id + col_id == rows - 1, 1.0, 0.0).astype(jnp.bfloat16)
    dq = dk = dv = None
    for head in range(2):
        weights = weight_ref[head]
        weight_grad = contract_cols(head_lanes(grad, head), value)
        product = weights * weight_grad
        centred = jnp.sum(product, axis=-1, keepdims=True)
        score_grad = (product - weights * centred).astype(jnp.bfloat16)
        part_v = head_lanes(contract_rows(weights.astype(jnp.bfloat16), grad), head)
        part_k = head_lanes(contract_rows(score_grad, query), head)
        part_q = head_lanes(
            jnp.dot(score_grad, key, preferred_element_type=jnp.float32), head
        )
        dv = part_v if dv is None else dv + part_v
        dk = part_k if dk is None else dk + part_k
        dq = part_q if dq is None else dq + part_q
        turned = jnp.dot(flip, score_grad, preferred_element_type=jnp.float32)
        wide = jnp.concatenate([turned, jnp.zeros((rows, rows), jnp.float32)], axis=1)
        skewed = pltpu.roll(wide, 0, 1, stride=1, stride_axis=0)
        offset_ref[0, head : head + 1, :] = jnp.sum(skewed, axis=0, keepdims=True)
    dq_ref[...] = dq.astype(jnp.bfloat16)
    dk_ref[...] = dk.astype(jnp.bfloat16)
    dv_ref[...] = dv.astype(jnp.bfloat16)


def attend_backward(projected, context_grad, weights):
    rows, width = projected.shape
    groups = width // 3 // 128
    col = lambda part: pl.BlockSpec((rows, 128), lambda g: (0, part * groups + g))
    grad_shape = jax.ShapeDtypeStruct((rows, width // 3), jnp.bfloat16)
    return pl.pallas_call(
        backward_kernel,
        grid=(groups,),
        in_specs=[
            col(0),
            col(1),
            col(2),
            col(0),
            pl.BlockSpec((2, rows, rows), lambda g: (g, 0, 0)),
        ],
        out_specs=[col(0), col(0), col(0), pl.BlockSpec((1, 2, 2 * rows), lambda g: (g, 0, 0))],
        out_shape=[grad_shape] * 3 + [jax.ShapeDtypeStruct((groups, 2, 2 * rows), jnp.float32)],
        compiler_params=pltpu.CompilerParams(vmem_limit_bytes=48 * 1024 * 1024),
        cost_estimate=pl.CostEstimate(
            flops=24 * groups * rows * rows * 128, bytes_accessed=2**24, transcendentals=0
        ),
    )(projected, projected, projected, context_grad, weights)


def per_device(
    tokens,
    attn_gain,
    qkv_weight,
    out_weight,
    ffn_gain,
    router_weight,
    inner_weight,
    outer_weight,
    bias_table,
    lengths,
    routes,
    buckets,
    out_cotangent,
):
    row_count, model_width = tokens.shape
    head_count = bias_table.shape[1]
    bucket_count = bias_table.shape[0]
    head_dim = model_width // head_count
    experts = inner_weight.shape[0]
    capacity = CAP
    both = ("dp", "fsdp")
    packed = jnp.concatenate(
        [
            qkv_weight,
            out_weight,
            attn_gain[:, None],
            ffn_gain[:, None],
            router_weight,
            jnp.zeros((attn_gain.shape[0], 128 - 2 - experts), jnp.bfloat16),
        ],
        axis=1,
    )
    packed_full = lax.all_gather(packed, both, axis=0, tiled=True)
    qkv_full = packed_full[:, : 3 * model_width]
    out_full = packed_full[:, 3 * model_width : 4 * model_width]
    gains_first = packed_full[:, 4 * model_width]
    gains_second = packed_full[:, 4 * model_width + 1]
    router_full = packed_full[:, 4 * model_width + 2 : 4 * model_width + 2 + experts]
    inner_full = lax.all_gather(inner_weight, both, axis=1, tiled=True)
    outer_full = lax.all_gather(outer_weight, both, axis=1, tiled=True)
    hidden_width = outer_full.shape[1]
    position = jnp.arange(row_count, dtype=jnp.int32)
    seq_ends = jnp.cumsum(lengths[0])
    segment = jnp.sum((position[:, None] >= seq_ends[None, :]).astype(jnp.int32), axis=1)
    live_rows = (position < seq_ends[-1]).astype(jnp.float32)[:, None]
    one_hot = (buckets[:, None] == jnp.arange(bucket_count, dtype=jnp.int32)[None, :]).astype(
        jnp.float32
    )
    offset_rows = lax.dot_general(
        bias_table,
        one_hot,
        (((0,), (1,)), ((), ())),
        precision=HIGHEST,
        preferred_element_type=jnp.float32,
    )
    inputs = tokens.astype(jnp.float32)
    first_gain = gains_first.astype(jnp.float32)
    normed = rms_scale(inputs, first_gain).astype(jnp.bfloat16)
    projected = jnp.dot(normed, qkv_full, preferred_element_type=jnp.float32).astype(jnp.bfloat16)

    offset_pad = jnp.pad(offset_rows, ((0, 0), (0, 1)))
    context, weights = attend_forward(projected, offset_pad, segment)
    attended = jnp.dot(context, out_full, preferred_element_type=jnp.float32)
    middle = inputs + live_rows * attended
    second_gain = gains_second.astype(jnp.float32)
    normed_two = rms_scale(middle, second_gain).astype(jnp.bfloat16)
    logits = jnp.dot(normed_two, router_full, preferred_element_type=jnp.float32)
    logit_top = jnp.max(logits, axis=1, keepdims=True)
    raised = jnp.exp(logits - logit_top)
    router_probs = raised / jnp.sum(raised, axis=1, keepdims=True)
    route_col = routes[:, 0]
    chosen = route_col[:, None] == jnp.arange(experts, dtype=jnp.int32)[None, :]
    chosen_weight = chosen.astype(jnp.float32)
    gating = jnp.sum(router_probs * chosen_weight, axis=1, keepdims=True)
    rank_in = jnp.cumsum(chosen.astype(jnp.int32), axis=0) - 1
    slot_of = jnp.sum(jnp.where(chosen, rank_in, 0), axis=1)
    slot_index = route_col * capacity + slot_of
    dispatch = (
        jnp.arange(experts * capacity, dtype=jnp.int32)[:, None] == slot_index[None, :]
    ).astype(jnp.bfloat16)

    def to_slots(rows):
        return jnp.dot(dispatch, rows, preferred_element_type=jnp.float32).astype(
            jnp.bfloat16
        ).reshape(experts, capacity, -1)

    def from_slots(rows):
        rows = rows.reshape(experts * capacity, -1)
        high = lax.reduce_precision(rows, 8, 7)
        low = (rows - high).astype(jnp.bfloat16)
        return contract_rows(dispatch, high.astype(jnp.bfloat16)) + contract_rows(dispatch, low)

    expert_rows = to_slots(normed_two)
    gate_up = jnp.einsum(
        "ecd,edf->ecf", expert_rows, inner_full, preferred_element_type=jnp.float32
    )
    activated = gated_unit(gate_up).astype(jnp.bfloat16)
    expert_out = jnp.einsum(
        "ecf,efd->ecd", activated, outer_full, preferred_element_type=jnp.float32
    )
    combined = from_slots(expert_out)
    mixed = (middle + live_rows * gating * combined).astype(jnp.bfloat16)
    first_back = gains_first.astype(jnp.float32)
    second_back = gains_second.astype(jnp.float32)
    cotangent = out_cotangent.astype(jnp.float32)
    branch_grad = live_rows * cotangent
    combined_grad = branch_grad * gating
    gating_grad = jnp.sum(branch_grad * combined, axis=1, keepdims=True)
    slot_grad = to_slots(combined_grad.astype(jnp.bfloat16))
    outer_sum = jnp.einsum("ecf,ecd->efd", activated, slot_grad, preferred_element_type=jnp.float32)
    act_grad = jnp.einsum("ecd,efd->ecf", slot_grad, outer_full, preferred_element_type=jnp.float32)
    unit_pull = jax.vjp(gated_unit, gate_up)[1]
    gate_up_grad = unit_pull(act_grad)[0].astype(jnp.bfloat16)
    inner_sum = [
        contract_rows(expert_rows[expert], gate_up_grad[expert]) for expert in range(experts)
    ]
    rows_grad = jnp.einsum(
        "ecf,edf->ecd", gate_up_grad, inner_full, preferred_element_type=jnp.float32
    )
    prob_grad = chosen_weight * gating_grad
    logit_grad = router_probs * (
        prob_grad - jnp.sum(router_probs * prob_grad, axis=1, keepdims=True)
    )
    router_sum = lax.dot_general(
        normed_two.astype(jnp.float32),
        logit_grad,
        (((0,), (0,)), ((), ())),
        precision=HIGHEST,
        preferred_element_type=jnp.float32,
    )
    normed_two_grad = from_slots(rows_grad) + lax.dot_general(
        logit_grad,
        router_full.astype(jnp.float32),
        (((1,), (1,)), ((), ())),
        precision=HIGHEST,
        preferred_element_type=jnp.float32,
    )
    norm_two_pull = jax.vjp(rms_scale, middle, second_back)[1]
    middle_part, second_gain_sum = norm_two_pull(normed_two_grad)
    middle_grad = cotangent + middle_part
    attended_grad = (live_rows * middle_grad).astype(jnp.bfloat16)
    out_sum = contract_rows(context, attended_grad)
    context_grad = contract_cols(attended_grad, out_full).astype(jnp.bfloat16)

    query_grad, key_grad, value_grad, offset_groups = attend_backward(
        projected, context_grad, weights
    )
    projected_grad = jnp.concatenate([query_grad, key_grad, value_grad], axis=1)
    qkv_sum = contract_rows(normed, projected_grad)
    normed_grad = contract_cols(projected_grad, qkv_full)
    norm_one_pull = jax.vjp(rms_scale, inputs, first_back)[1]
    input_part, first_gain_sum = norm_one_pull(normed_grad)
    tokens_grad = middle_grad + input_part
    offset_grad = offset_groups.reshape(head_count, -1)[:, : buckets.shape[0]]
    table_part = lax.dot_general(
        one_hot,
        offset_grad,
        (((0,), (1,)), ((), ())),
        precision=HIGHEST,
        preferred_element_type=jnp.float32,
    )
    def scatter(partial_sum, axis):
        low = partial_sum.astype(jnp.bfloat16)
        return lax.psum_scatter(low, both, scatter_dimension=axis, tiled=True).astype(jnp.float32)

    inner_grad = jnp.stack([scatter(inner_part, 0) for inner_part in inner_sum])
    outer_grad = scatter(outer_sum, 1)
    qkv_out = scatter(jnp.concatenate([qkv_sum, out_sum], axis=1), 0)
    qkv_weight_grad = qkv_out[:, : 3 * model_width]
    out_weight_grad = qkv_out[:, 3 * model_width :]
    small = jnp.concatenate(
        [
            first_gain_sum,
            second_gain_sum,
            jnp.transpose(router_sum).reshape(-1),
            table_part.reshape(-1),
        ]
    )
    small = lax.psum(small.reshape(-1, 128), both).reshape(-1)
    own_rows = attn_gain.shape[0]
    first_own = (lax.axis_index("dp") * lax.axis_size("fsdp") + lax.axis_index("fsdp")) * own_rows
    columns = small[: (2 + experts) * model_width].reshape(2 + experts, model_width)
    columns = lax.dynamic_slice_in_dim(columns, first_own, own_rows, 1)
    attn_gain_grad = columns[0]
    ffn_gain_grad = columns[1]
    router_grad = jnp.transpose(columns[2:])
    table_grad = small[(2 + experts) * model_width :].reshape(bucket_count, head_count)
    return (
        mixed,
        tokens_grad,
        attn_gain_grad,
        qkv_weight_grad,
        out_weight_grad,
        ffn_gain_grad,
        router_grad,
        inner_grad,
        outer_grad,
        table_grad,
    )


def solution(mesh):
    placed = (
        P(("dp", "fsdp"), None),
        P(("dp", "fsdp")),
        P(("dp", "fsdp"), None),
        P(("dp", "fsdp"), None),
        P(("dp", "fsdp")),
        P(("dp", "fsdp"), None),
        P(None, ("dp", "fsdp"), None),
        P(None, ("dp", "fsdp"), None),
        P(),
        P(("dp", "fsdp"), None),
        P(("dp", "fsdp"), None),
        P(),
        P(("dp", "fsdp"), None),
    )
    return jax.shard_map(
        per_device,
        mesh=mesh,
        in_specs=placed,
        out_specs=(
            P(("dp", "fsdp"), None),
            P(("dp", "fsdp"), None),
            P(("dp", "fsdp")),
            P(("dp", "fsdp"), None),
            P(("dp", "fsdp"), None),
            P(("dp", "fsdp")),
            P(("dp", "fsdp"), None),
            P(None, ("dp", "fsdp"), None),
            P(None, ("dp", "fsdp"), None),
            P(),
        ),
        check_vma=False,
    )
```

```python
import jax
import jax.numpy as jnp
from jax import lax
from jax.experimental import pallas as pl
from jax.experimental.pallas import tpu as pltpu
from jax.sharding import PartitionSpec as P

CAP = 320
HEAD_DIM = 64


EPSILON = 1e-06
NEGATIVE = -1e30
HIGHEST = lax.Precision.HIGHEST


def rms_scale(values, gain_row):
    return (
        values * lax.rsqrt(jnp.mean(values * values, axis=-1, keepdims=True) + EPSILON) * gain_row
    )


def gated_unit(gate_up):
    hidden_units = gate_up.shape[-1] // 2
    return jax.nn.gelu(gate_up[..., :hidden_units], approximate=True) * gate_up[..., hidden_units:]


def contract_rows(left_side, right_side):
    return lax.dot_general(
        left_side, right_side, (((0,), (0,)), ((), ())), preferred_element_type=jnp.float32
    )


def contract_cols(left_side, right_side):
    return lax.dot_general(
        left_side, right_side, (((1,), (1,)), ((), ())), preferred_element_type=jnp.float32
    )


def head_lanes(values, head):
    lane = lax.broadcasted_iota(jnp.int32, values.shape, 1)
    return jnp.where((lane // HEAD_DIM) == head, values, jnp.zeros_like(values))


def forward_kernel(query_ref, key_ref, value_ref, offset_ref, seg_col_ref, seg_row_ref, context_ref, weight_ref):
    rows = query_ref.shape[0]
    same_doc = seg_col_ref[...] == seg_row_ref[...]
    query, key, value = query_ref[...], key_ref[...], value_ref[...]
    context = None
    for head in range(2):
        wide = jnp.broadcast_to(offset_ref[0, head : head + 1, :], (rows, 2 * rows))
        bias = pltpu.roll(wide, rows + 1, 1, stride=1, stride_axis=0)[:, :rows]
        scores = contract_cols(head_lanes(query, head), key) + bias
        scores = jnp.where(same_doc, scores, NEGATIVE)
        highest = jnp.max(scores, axis=-1, keepdims=True)
        raised = jnp.exp(scores - highest)
        weights = raised / jnp.sum(raised, axis=-1, keepdims=True)
        weight_ref[head] = weights
        part = jnp.dot(weights.astype(jnp.bfloat16), value, preferred_element_type=jnp.float32)
        part = head_lanes(part, head)
        context = part if context is None else context + part
    context_ref[...] = context.astype(jnp.bfloat16)


def attend_forward(projected, offset_pad, segment):
    rows, width = projected.shape
    groups = width // 3 // 128
    col = lambda part: pl.BlockSpec((rows, 128), lambda g: (0, part * groups + g))
    return pl.pallas_call(
        forward_kernel,
        grid=(groups,),
        in_specs=[
            col(0),
            col(1),
            col(2),
            pl.BlockSpec((1, 2, 2 * rows), lambda g: (g, 0, 0)),
            pl.BlockSpec((rows, 1), lambda g: (0, 0)),
            pl.BlockSpec((1, rows), lambda g: (0, 0)),
        ],
        out_specs=[
            pl.BlockSpec((rows, 128), lambda g: (0, g)),
            pl.BlockSpec((2, rows, rows), lambda g: (g, 0, 0)),
        ],
        out_shape=[
            jax.ShapeDtypeStruct((rows, width // 3), jnp.bfloat16),
            jax.ShapeDtypeStruct((2 * groups, rows, rows), jnp.float32),
        ],
        compiler_params=pltpu.CompilerParams(vmem_limit_bytes=48 * 1024 * 1024),
        cost_estimate=pl.CostEstimate(
            flops=8 * groups * rows * rows * 128, bytes_accessed=2**24, transcendentals=2**22
        ),
    )(
        projected,
        projected,
        projected,
        offset_pad.reshape(groups, 2, 2 * rows),
        segment[:, None],
        segment[None, :],
    )


def backward_kernel(
    query_ref, key_ref, value_ref, grad_ref, weight_ref, dq_ref, dk_ref, dv_ref, offset_ref
):
    rows = query_ref.shape[0]
    query, key, value, grad = query_ref[...], key_ref[...], value_ref[...], grad_ref[...]
    row_id = lax.broadcasted_iota(jnp.int32, (rows, rows), 0)
    col_id = lax.broadcasted_iota(jnp.int32, (rows, rows), 1)
    flip = jnp.where(row_id + col_id == rows - 1, 1.0, 0.0).astype(jnp.bfloat16)
    dq = dk = dv = None
    for head in range(2):
        weights = weight_ref[head]
        weight_grad = contract_cols(head_lanes(grad, head), value)
        product = weights * weight_grad
        centred = jnp.sum(product, axis=-1, keepdims=True)
        score_grad = (product - weights * centred).astype(jnp.bfloat16)
        part_v = head_lanes(contract_rows(weights.astype(jnp.bfloat16), grad), head)
        part_k = head_lanes(contract_rows(score_grad, query), head)
        part_q = head_lanes(
            jnp.dot(score_grad, key, preferred_element_type=jnp.float32), head
        )
        dv = part_v if dv is None else dv + part_v
        dk = part_k if dk is None else dk + part_k
        dq = part_q if dq is None else dq + part_q
        turned = jnp.dot(flip, score_grad, preferred_element_type=jnp.float32)
        wide = jnp.concatenate([turned, jnp.zeros((rows, rows), jnp.float32)], axis=1)
        skewed = pltpu.roll(wide, 0, 1, stride=1, stride_axis=0)
        offset_ref[0, head : head + 1, :] = jnp.sum(skewed, axis=0, keepdims=True)
    dq_ref[...] = dq.astype(jnp.bfloat16)
    dk_ref[...] = dk.astype(jnp.bfloat16)
    dv_ref[...] = dv.astype(jnp.bfloat16)


def attend_backward(projected, context_grad, weights):
    rows, width = projected.shape
    groups = width // 3 // 128
    col = lambda part: pl.BlockSpec((rows, 128), lambda g: (0, part * groups + g))
    grad_shape = jax.ShapeDtypeStruct((rows, width // 3), jnp.bfloat16)
    return pl.pallas_call(
        backward_kernel,
        grid=(groups,),
        in_specs=[
            col(0),
            col(1),
            col(2),
            col(0),
            pl.BlockSpec((2, rows, rows), lambda g: (g, 0, 0)),
        ],
        out_specs=[col(0), col(0), col(0), pl.BlockSpec((1, 2, 2 * rows), lambda g: (g, 0, 0))],
        out_shape=[grad_shape] * 3 + [jax.ShapeDtypeStruct((groups, 2, 2 * rows), jnp.float32)],
        compiler_params=pltpu.CompilerParams(vmem_limit_bytes=48 * 1024 * 1024),
        cost_estimate=pl.CostEstimate(
            flops=24 * groups * rows * rows * 128, bytes_accessed=2**24, transcendentals=0
        ),
    )(projected, projected, projected, context_grad, weights)


def device_bits():
    bits = []
    for axis in ("dp", "fsdp"):
        span = lax.axis_size(axis) // 2
        while span:
            bits.append((axis, span))
            span //= 2
    return bits


def swap_bit(values, bit):
    axis, span = bit
    pairs = [(source, source ^ span) for source in range(lax.axis_size(axis))]
    return lax.ppermute(values, axis, pairs)


def own_bit(bit):
    axis, span = bit
    return (lax.axis_index(axis) // span) % 2


def stage_order(turn):
    bits = device_bits()
    outer = list(range(len(bits) - 1))
    first = {0: ("fsdp", 2), 1: ("dp", 1), 2: ("dp", 2), 3: ("dp", 1)}[turn]
    begin = bits.index(first) if first in bits else 0
    order = [(begin - step) % len(outer) for step in range(len(outer))]
    return [len(bits) - 1] + order


def halving_sum(partial_sum, turn):

    bits = device_bits()
    tail = partial_sum.shape[1:]
    values = partial_sum.reshape([2] * len(bits) + list(tail))
    order = stage_order(turn)
    for place in order:
        side = own_bit(bits[place])
        sent = lax.dynamic_slice_in_dim(values, 1 - side, 1, place)
        kept = lax.dynamic_slice_in_dim(values, side, 1, place)
        got = swap_bit(sent, bits[place])
        values = kept.astype(jnp.float32) + got.astype(jnp.float32)
        if place != order[-1]:
            values = values.astype(jnp.bfloat16)
    return values.reshape(tail)


def doubling_gather(own, turn):

    bits = device_bits()
    experts, rows, columns = own.shape
    values = own.reshape([experts] + [1] * len(bits) + [rows, columns])
    for place in reversed(stage_order(turn)):
        side = own_bit(bits[place])
        got = swap_bit(values, bits[place])
        lower = jnp.where(side == 0, values, got)
        upper = jnp.where(side == 0, got, values)
        values = jnp.concatenate([lower, upper], axis=1 + place)
    return values.reshape(experts, -1, columns)


def per_device(
    tokens,
    attn_gain,
    qkv_weight,
    out_weight,
    ffn_gain,
    router_weight,
    inner_weight,
    outer_weight,
    bias_table,
    lengths,
    routes,
    buckets,
    out_cotangent,
):
    row_count, model_width = tokens.shape
    head_count = bias_table.shape[1]
    bucket_count = bias_table.shape[0]
    head_dim = model_width // head_count
    experts = inner_weight.shape[0]
    capacity = CAP
    both = ("dp", "fsdp")
    devices = lax.axis_size("dp") * lax.axis_size("fsdp")
    packed = jnp.concatenate(
        [
            qkv_weight,
            out_weight,
            attn_gain[:, None],
            ffn_gain[:, None],
            router_weight,
            jnp.zeros((attn_gain.shape[0], 128 - 2 - experts), jnp.bfloat16),
        ],
        axis=1,
    )
    packed_full = lax.all_gather(packed, both, axis=0, tiled=True)
    qkv_full = packed_full[:, : 3 * model_width]
    out_full = packed_full[:, 3 * model_width : 4 * model_width]
    gains_first = packed_full[:, 4 * model_width]
    gains_second = packed_full[:, 4 * model_width + 1]
    router_full = packed_full[:, 4 * model_width + 2 : 4 * model_width + 2 + experts]
    inner_full = lax.all_gather(inner_weight, both, axis=1, tiled=True)
    outer_full = doubling_gather(outer_weight, 0)
    hidden_width = outer_full.shape[1]
    position = jnp.arange(row_count, dtype=jnp.int32)
    seq_ends = jnp.cumsum(lengths[0])
    segment = jnp.sum((position[:, None] >= seq_ends[None, :]).astype(jnp.int32), axis=1)
    live_rows = (position < seq_ends[-1]).astype(jnp.float32)[:, None]
    one_hot = (buckets[:, None] == jnp.arange(bucket_count, dtype=jnp.int32)[None, :]).astype(
        jnp.float32
    )
    offset_rows = lax.dot_general(
        bias_table,
        one_hot,
        (((0,), (1,)), ((), ())),
        precision=HIGHEST,
        preferred_element_type=jnp.float32,
    )
    inputs = tokens.astype(jnp.float32)
    first_gain = gains_first.astype(jnp.float32)
    normed = rms_scale(inputs, first_gain).astype(jnp.bfloat16)
    projected = jnp.dot(normed, qkv_full, preferred_element_type=jnp.float32).astype(jnp.bfloat16)

    offset_pad = jnp.pad(offset_rows, ((0, 0), (0, 1)))
    context, weights = attend_forward(projected, offset_pad, segment)
    attended = jnp.dot(context, out_full, preferred_element_type=jnp.float32)
    middle = inputs + live_rows * attended
    second_gain = gains_second.astype(jnp.float32)
    normed_two = rms_scale(middle, second_gain).astype(jnp.bfloat16)
    logits = jnp.dot(normed_two, router_full, preferred_element_type=jnp.float32)
    logit_top = jnp.max(logits, axis=1, keepdims=True)
    raised = jnp.exp(logits - logit_top)
    router_probs = raised / jnp.sum(raised, axis=1, keepdims=True)
    route_col = routes[:, 0]
    chosen = route_col[:, None] == jnp.arange(experts, dtype=jnp.int32)[None, :]
    chosen_weight = chosen.astype(jnp.float32)
    gating = jnp.sum(router_probs * chosen_weight, axis=1, keepdims=True)
    rank_in = jnp.cumsum(chosen.astype(jnp.int32), axis=0) - 1
    slot_of = jnp.sum(jnp.where(chosen, rank_in, 0), axis=1)
    slot_index = route_col * capacity + slot_of
    dispatch = (
        jnp.arange(experts * capacity, dtype=jnp.int32)[:, None] == slot_index[None, :]
    ).astype(jnp.bfloat16)

    def to_slots(rows):
        return jnp.dot(dispatch, rows, preferred_element_type=jnp.float32).astype(
            jnp.bfloat16
        ).reshape(experts, capacity, -1)

    def from_slots(rows):
        rows = rows.reshape(experts * capacity, -1)
        high = lax.reduce_precision(rows, 8, 7)
        low = (rows - high).astype(jnp.bfloat16)
        return contract_rows(dispatch, high.astype(jnp.bfloat16)) + contract_rows(dispatch, low)

    expert_rows = to_slots(normed_two)
    gate_up = jnp.einsum(
        "ecd,edf->ecf", expert_rows, inner_full, preferred_element_type=jnp.float32
    )
    activated = gated_unit(gate_up).astype(jnp.bfloat16)
    expert_out = jnp.einsum(
        "ecf,efd->ecd", activated, outer_full, preferred_element_type=jnp.float32
    )
    combined = from_slots(expert_out)
    mixed = (middle + live_rows * gating * combined).astype(jnp.bfloat16)
    first_back = gains_first.astype(jnp.float32)
    second_back = gains_second.astype(jnp.float32)
    cotangent = out_cotangent.astype(jnp.float32)
    branch_grad = live_rows * cotangent
    combined_grad = branch_grad * gating
    gating_grad = jnp.sum(branch_grad * combined, axis=1, keepdims=True)
    slot_grad = to_slots(combined_grad.astype(jnp.bfloat16))
    outer_sum = jnp.einsum("ecf,ecd->efd", activated, slot_grad, preferred_element_type=jnp.float32)
    act_grad = jnp.einsum("ecd,efd->ecf", slot_grad, outer_full, preferred_element_type=jnp.float32)
    unit_pull = jax.vjp(gated_unit, gate_up)[1]
    gate_up_grad = unit_pull(act_grad)[0].astype(jnp.bfloat16)
    inner_sum = [
        contract_rows(expert_rows[expert], gate_up_grad[expert]) for expert in range(experts)
    ]
    def by_owner(partial_sum):
        return partial_sum.astype(jnp.bfloat16).reshape(devices, -1, partial_sum.shape[-1])

    outer_low = jnp.concatenate(
        [outer_sum[expert].astype(jnp.bfloat16).reshape(devices, -1, model_width) for expert in range(experts)],
        axis=1,
    )
    outer_grad = halving_sum(outer_low, 0).reshape(experts, -1, model_width)
    inner_low = [by_owner(inner_part) for inner_part in inner_sum]
    inner_grad = jnp.stack(
        [halving_sum(inner_low[expert], 1 + expert % 2) for expert in range(experts)]
    )
    rows_grad = jnp.einsum(
        "ecf,edf->ecd", gate_up_grad, inner_full, preferred_element_type=jnp.float32
    )
    prob_grad = chosen_weight * gating_grad
    logit_grad = router_probs * (
        prob_grad - jnp.sum(router_probs * prob_grad, axis=1, keepdims=True)
    )
    router_sum = lax.dot_general(
        normed_two.astype(jnp.float32),
        logit_grad,
        (((0,), (0,)), ((), ())),
        precision=HIGHEST,
        preferred_element_type=jnp.float32,
    )
    normed_two_grad = from_slots(rows_grad) + lax.dot_general(
        logit_grad,
        router_full.astype(jnp.float32),
        (((1,), (1,)), ((), ())),
        precision=HIGHEST,
        preferred_element_type=jnp.float32,
    )
    norm_two_pull = jax.vjp(rms_scale, middle, second_back)[1]
    middle_part, second_gain_sum = norm_two_pull(normed_two_grad)
    middle_grad = cotangent + middle_part
    attended_grad = (live_rows * middle_grad).astype(jnp.bfloat16)
    attended_grad, *_ = lax.optimization_barrier((attended_grad, outer_low, *inner_low))
    out_sum = contract_rows(context, attended_grad)
    context_grad = contract_cols(attended_grad, out_full).astype(jnp.bfloat16)

    query_grad, key_grad, value_grad, offset_groups = attend_backward(
        projected, context_grad, weights
    )
    projected_grad = jnp.concatenate([query_grad, key_grad, value_grad], axis=1)
    qkv_sum = contract_rows(normed, projected_grad)
    normed_grad = contract_cols(projected_grad, qkv_full)
    norm_one_pull = jax.vjp(rms_scale, inputs, first_back)[1]
    input_part, first_gain_sum = norm_one_pull(normed_grad)
    tokens_grad = middle_grad + input_part
    offset_grad = offset_groups.reshape(head_count, -1)[:, : buckets.shape[0]]
    table_part = lax.dot_general(
        one_hot,
        offset_grad,
        (((0,), (1,)), ((), ())),
        precision=HIGHEST,
        preferred_element_type=jnp.float32,
    )
    qkv_out = halving_sum(by_owner(jnp.concatenate([qkv_sum, out_sum], axis=1)), 3)
    qkv_weight_grad = qkv_out[:, : 3 * model_width]
    out_weight_grad = qkv_out[:, 3 * model_width :]
    small = jnp.concatenate(
        [
            first_gain_sum,
            second_gain_sum,
            jnp.transpose(router_sum).reshape(-1),
            table_part.reshape(-1),
        ]
    )
    small = lax.psum(small.reshape(-1, 128), both).reshape(-1)
    own_rows = attn_gain.shape[0]
    first_own = (lax.axis_index("dp") * lax.axis_size("fsdp") + lax.axis_index("fsdp")) * own_rows
    columns = small[: (2 + experts) * model_width].reshape(2 + experts, model_width)
    columns = lax.dynamic_slice_in_dim(columns, first_own, own_rows, 1)
    attn_gain_grad = columns[0]
    ffn_gain_grad = columns[1]
    router_grad = jnp.transpose(columns[2:])
    table_grad = small[(2 + experts) * model_width :].reshape(bucket_count, head_count)
    return (
        mixed,
        tokens_grad,
        attn_gain_grad,
        qkv_weight_grad,
        out_weight_grad,
        ffn_gain_grad,
        router_grad,
        inner_grad,
        outer_grad,
        table_grad,
    )


def solution(mesh):
    placed = (
        P(("dp", "fsdp"), None),
        P(("dp", "fsdp")),
        P(("dp", "fsdp"), None),
        P(("dp", "fsdp"), None),
        P(("dp", "fsdp")),
        P(("dp", "fsdp"), None),
        P(None, ("dp", "fsdp"), None),
        P(None, ("dp", "fsdp"), None),
        P(),
        P(("dp", "fsdp"), None),
        P(("dp", "fsdp"), None),
        P(),
        P(("dp", "fsdp"), None),
    )
    return jax.shard_map(
        per_device,
        mesh=mesh,
        in_specs=placed,
        out_specs=(
            P(("dp", "fsdp"), None),
            P(("dp", "fsdp"), None),
            P(("dp", "fsdp")),
            P(("dp", "fsdp"), None),
            P(("dp", "fsdp"), None),
            P(("dp", "fsdp")),
            P(("dp", "fsdp"), None),
            P(None, ("dp", "fsdp"), None),
            P(None, ("dp", "fsdp"), None),
            P(),
        ),
        check_vma=False,
    )
```
